128 devices in a mesh: dap: 8 (over z, y_lo), samp: 16 (over x, y_hi, core).
Axes of the slice: x: 4, y: 4 (y_hi: 2, y_lo: 2; y = y_hi * 2 + y_lo), z: 4, core: 2. Of those that a mesh axis runs over, the one named last changes fastest.
Arguments:
- pair_rep: bfloat16 [512, 512, 128], P('dap', 'samp'), may hold values from -6 to 6
- single: bfloat16 [512, 384], P('dap'), may hold values from -6 to 6
- residue_type: int32 [512], replicated, may hold values from 0 to 31
- chain_id: int32 [512], replicated, may hold values from 0 to 3, never falling along the last dimension, each value on 1 to 256 neighbouring positions
- residue_index: int32 [512], replicated, may hold values from 1 to 1024, as said below
- noisy_pos: float32 [64, 3, 512], P('samp', None, 'dap'), may hold values from -6 to 6
- type_table: bfloat16 [32, 384], replicated, may hold values from -6 to 6
- relpos_table: bfloat16 [66, 128], replicated, may hold values from -6 to 6
- tri_proj: bfloat16 [128, 512], replicated, may hold values from -0.5 to 0.5
- tri_gate: bfloat16 [128, 128], replicated, may hold values from -0.5 to 0.5
- tri_out: bfloat16 [128, 128], replicated, may hold values from -0.5 to 0.5
- bias_proj: bfloat16 [128, 16], replicated
- single_proj: bfloat16 [384, 768], replicated, may hold values from -0.3125 to 0.3125
- pos_proj: float32 [3, 768], replicated, may hold values from -3.5 to 3.5
- attn_proj: bfloat16 [768, 3072], replicated, may hold values from -0.21875 to 0.21875
- attn_out: bfloat16 [768, 768], replicated, may hold values from -0.21875 to 0.21875
- ff_in: bfloat16 [768, 3072], replicated, may hold values from -0.21875 to 0.21875
- ff_out: bfloat16 [1536, 768], replicated, may hold values from -0.15625 to 0.15625
- coord_out: bfloat16 [3, 768], replicated, may hold values from -0.21875 to 0.21875
Outputs:
- pair_next: bfloat16 [512, 512, 128], P('dap', 'samp')
- positions: float32 [64, 3, 512], P('samp', None, 'dap')
The draws below stay inside these ranges and needn't reach their ends.
Inputs may be any that keep to these rules, and one draw needn't show every extreme that they name: `residue_index`: rises by 1 to 3 from each token to the next. `chain_id`: never falls along the tokens.
All inputs are finite; a program needn't handle non-finite values.
Results may differ from the reference program's by a relative error of at most 0.0094.
Values may be sent and summed in bfloat16 or wider, within the bound.
No kernel may reach another device: no remote copies, remote signals or barrier semaphores. Data moves between devices by JAX's collectives and lax.ppermute only.
A program may use at most 128 MiB of HBM per device.

```python
import math
import jax
import jax.numpy as jnp
import numpy as np
from jax import lax

C = 128
TRI = 128
CS = 384
CA = 768
HEADS = 16
FFN = 1536
HEAD = 48
BINS = 66
TYPES = 32
TOK_DEV = 64
TOKENS = 512
SAMPLES = 64
N_DAP = 8


def draw_residue_index(key, part):
    key = jax.random.fold_in(key, 11)
    flags = jax.random.randint(key, (TOKENS,), 0, 2, dtype=jnp.int32)
    positions_here = jnp.arange(TOKENS, dtype=jnp.int32)
    flags = jnp.where(positions_here == 0, 0, flags)
    flags = jnp.where(positions_here == TOKENS - 1, 1, flags)
    return (2 * positions_here + 1 + flags).astype(jnp.int32)


def draw_bias_proj(key, part):
    key = jax.random.fold_in(key, 5)
    key_base, key_scale = jax.random.split(key)
    base = jax.random.normal(key_base, (C, HEADS), jnp.float32)
    scales = jnp.exp(jax.random.uniform(key_scale, (HEADS,), jnp.float32, -0.7, 0.7))
    return (base * scales[None, :] / jnp.sqrt(jnp.float32(C))).astype(jnp.bfloat16)


def set_ends(drawn, own_key, least, top_value):
    dims = drawn.shape
    place = [jax.random.randint(jax.random.fold_in(own_key, axis), (), 0, dims[axis]) for axis in range(len(dims))]
    drawn = drawn.at[tuple(place)].set(least)
    longest = dims.index(max(dims))
    place[longest] = (place[longest] + 1) % dims[longest]
    return drawn.at[tuple(place)].set(top_value)


def block_levels(own_key, extent, pieces, low, high):
    loudness, own = 1.0, jax.random.fold_in(own_key, 6)
    for dim, parts in pieces:
        steps = jnp.exp(jax.random.uniform(jax.random.fold_in(own, dim), (parts,), jnp.float32, low / len(pieces), high / len(pieces)))
        loudness = loudness * jnp.repeat(steps, extent[dim] // parts).reshape([-1 if axis == dim else 1 for axis in range(len(extent))])
    return loudness


def split_up(amount, total, limit, skew):
    loads = [(1 << 20) // math.isqrt(grade ** skew) + 1 for grade in range(2, amount + 1)]
    spare, given = total - limit - (amount - 1), [1] * (amount - 1)
    while spare > 0:
        candidates = [i for i in range(amount - 1) if given[i] < limit]
        mass, budget = sum([loads[i] for i in candidates]), spare
        for i in candidates:
            more = min(limit - given[i], max(1, budget * loads[i] // mass), spare)
            given[i] = given[i] + more
            spare = spare - more
    return np.array([limit] + given)


def uneven_parts(rng, count, total, reach, slope):
    if count == 2:
        one = jax.random.randint(rng, (), max(1, total - reach), min(reach, total - 1) + 1)
        return jnp.stack([one, total - one])
    tallies = jnp.asarray(split_up(count, total, reach, slope), jnp.int32)
    pairs = (count - 1) // 2
    giver, sink = tallies[1:1 + 2 * pairs:2], tallies[2:2 + 2 * pairs:2]
    room = jnp.minimum(giver - 1, reach - sink)
    moved = jax.random.randint(jax.random.fold_in(rng, 1), (pairs,), 0, 1 << 20) % (room + 1)
    tallies = tallies.at[1:1 + 2 * pairs:2].set(giver - moved).at[2:2 + 2 * pairs:2].set(sink + moved)
    return tallies[jax.random.permutation(jax.random.fold_in(rng, 2), count)]


def normal_values(rng, extent, scale, limit, cuts=(), kind=jnp.bfloat16):
    array = jax.random.normal(rng, extent, jnp.float32) * scale
    if len(cuts) > 0:
        array = block_levels(rng, extent, cuts, -0.22, 0.18) * array
    return jnp.clip(array, min=-limit, max=limit).astype(kind)


def setup_inputs(seed: int = 0) -> dict:
    seeds = jax.random.split(jax.random.key(seed), 20)
    return {
        "pair_rep": normal_values(seeds[0], (TOKENS, TOKENS, C), 1.0, 6.0, ((0, 8), (1, 16))),
        "single": normal_values(seeds[1], (TOKENS, CS), 1.0, 6.0, ((0, 8),)),
        "residue_type": set_ends(jax.random.randint(seeds[2], (TOKENS,), 0, TYPES), jax.random.fold_in(seeds[2], 1), 0, TYPES - 1).astype(jnp.int32),
        "chain_id": jnp.searchsorted(jnp.cumsum(uneven_parts(seeds[3], 4, TOKENS, TOKENS // 2, 1)), jnp.arange(TOKENS), side="right").astype(jnp.int32),
        "residue_index": draw_residue_index(jax.random.fold_in(seeds[19], 71), 0),
        "noisy_pos": normal_values(seeds[5], (SAMPLES, 3, TOKENS), 1.0, 6.0, ((0, 16), (2, 8)), jnp.float32),
        "type_table": normal_values(seeds[6], (TYPES, CS), 1.0, 6.0),
        "relpos_table": normal_values(seeds[7], (BINS, C), 1.0, 6.0),
        "tri_proj": normal_values(seeds[8], (C, 4 * TRI), C ** -0.5, 0.5),
        "tri_gate": normal_values(seeds[9], (C, C), C ** -0.5, 0.5),
        "tri_out": normal_values(seeds[10], (TRI, C), TRI ** -0.5, 0.5),
        "bias_proj": draw_bias_proj(jax.random.fold_in(seeds[19], 71), 0),
        "single_proj": normal_values(seeds[12], (CS, CA), CS ** -0.5, 0.3125),
        "pos_proj": normal_values(seeds[13], (3, CA), 3 ** -0.5, 3.5, (), jnp.float32),
        "attn_proj": normal_values(seeds[14], (CA, 4 * CA), CA ** -0.5, 0.21875),
        "attn_out": normal_values(seeds[15], (CA, CA), CA ** -0.5, 0.21875),
        "ff_in": normal_values(seeds[16], (CA, 2 * FFN), CA ** -0.5, 0.21875),
        "ff_out": normal_values(seeds[17], (FFN, CA), FFN ** -0.5, 0.15625),
        "coord_out": normal_values(seeds[18], (3, CA), CA ** -0.5, 0.21875),
    }


def layer_norm(values):
    center = values - lax.optimization_barrier(jnp.mean(values, axis=-1, keepdims=True))
    spread = lax.optimization_barrier(jnp.mean(center * center, axis=-1, keepdims=True))
    return center * lax.rsqrt(spread + 1e-05)

def relative_bins(index_rows, index_cols, chain_rows, chain_cols):
    offset = jnp.clip(index_rows[:, None] - index_cols[None, :], -32, 32) + 32
    return jnp.where(chain_rows[:, None] == chain_cols[None, :], offset, 65).astype(jnp.int32)

def reference(pair_rep, single, residue_type, chain_id, residue_index, noisy_pos, type_table, relpos_table, tri_proj, tri_gate, tri_out, bias_proj, single_proj, pos_proj, attn_proj, attn_out, ff_in, ff_out, coord_out):
    bins = relative_bins(residue_index, residue_index, chain_id, chain_id)
    embed = jnp.take(relpos_table.astype(jnp.float32), bins, axis=0)
    pair_in = pair_rep.astype(jnp.float32) + embed
    pair_norm = layer_norm(pair_in).astype(jnp.bfloat16)
    projected = jnp.dot(pair_norm.reshape(-1, C), tri_proj, preferred_element_type=jnp.float32).reshape(TOKENS, TOKENS, 4 * TRI)
    left = (jax.nn.sigmoid(projected[..., TRI:2 * TRI]) * projected[..., :TRI]).astype(jnp.bfloat16)
    right = (jax.nn.sigmoid(projected[..., 3 * TRI:]) * projected[..., 2 * TRI:3 * TRI]).astype(jnp.bfloat16)
    right_wide = right.astype(jnp.float32)

    def row_block(start):
        left_rows = lax.dynamic_slice_in_dim(left, start, TOK_DEV, 0).astype(jnp.float32)
        return jnp.einsum('ikc,jkc->ijc', left_rows, right_wide)
    starts = jnp.arange(N_DAP, dtype=jnp.int32) * TOK_DEV
    tri_sum = lax.map(row_block, starts).reshape(TOKENS, TOKENS, TRI)
    tri_norm = layer_norm(tri_sum).astype(jnp.bfloat16)
    update = jnp.dot(tri_norm.reshape(-1, TRI), tri_out, preferred_element_type=jnp.float32).reshape(TOKENS, TOKENS, C)
    gating = jax.nn.sigmoid(jnp.dot(pair_norm.reshape(-1, C), tri_gate, preferred_element_type=jnp.float32)).reshape(TOKENS, TOKENS, C)
    pair_next = (pair_in + gating * update).astype(jnp.bfloat16)
    bias_norm = layer_norm(pair_next.astype(jnp.float32)).astype(jnp.bfloat16)
    pair_bias = jnp.dot(bias_norm.reshape(-1, C), bias_proj, preferred_element_type=jnp.float32).reshape(TOKENS, TOKENS, HEADS).transpose(2, 0, 1)
    token_feat = single.astype(jnp.float32) + jnp.take(type_table.astype(jnp.float32), residue_type, axis=0)
    condition = jnp.dot(layer_norm(token_feat).astype(jnp.bfloat16), single_proj, preferred_element_type=jnp.float32)

    def one_sample(coords):
        act = condition + jnp.einsum('cn,ct->nt', coords, pos_proj, precision=lax.Precision.HIGHEST)
        normed = layer_norm(act).astype(jnp.bfloat16)
        mixed = jnp.dot(normed, attn_proj, preferred_element_type=jnp.float32)
        query = mixed[:, :CA].astype(jnp.bfloat16).reshape(TOKENS, HEADS, HEAD)
        key_part = mixed[:, CA:2 * CA].astype(jnp.bfloat16).reshape(TOKENS, HEADS, HEAD)
        value_part = mixed[:, 2 * CA:3 * CA].astype(jnp.bfloat16).reshape(TOKENS, HEADS, HEAD)
        gates = jax.nn.sigmoid(mixed[:, 3 * CA:])
        scores = jnp.einsum('qhd,khd->hqk', query.astype(jnp.float32), key_part.astype(jnp.float32)) * HEAD ** (-0.5) + pair_bias
        weights = jax.nn.softmax(scores, axis=-1).astype(jnp.bfloat16)
        attended = jnp.einsum('hqk,khd->qhd', weights.astype(jnp.float32), value_part.astype(jnp.float32)).reshape(TOKENS, CA)
        gated = (gates * attended).astype(jnp.bfloat16)
        act = act + jnp.dot(gated, attn_out, preferred_element_type=jnp.float32)
        hidden = jnp.dot(layer_norm(act).astype(jnp.bfloat16), ff_in, preferred_element_type=jnp.float32)
        inner = (jax.nn.silu(hidden[:, :FFN]) * hidden[:, FFN:]).astype(jnp.bfloat16)
        act = act + jnp.dot(inner, ff_out, preferred_element_type=jnp.float32)
        final = layer_norm(act).astype(jnp.bfloat16)
        shift = jnp.einsum('ct,nt->cn', coord_out.astype(jnp.float32), final.astype(jnp.float32))
        return coords + shift
    positions = lax.map(one_sample, noisy_pos)
    return (pair_next, positions)
```

```python
import jax
import jax.numpy as jnp
from jax import lax
from jax.experimental import pallas as pl
from jax.experimental.pallas import tpu as pltpu
from jax.sharding import Mesh, PartitionSpec as P

F32 = jnp.float32
BF16 = jnp.bfloat16
AXES = ("dap", "sch", "core")
LOG2E = 1.4426950408889634
MIB = 1024 * 1024


def dot(a, b, dims):
    return lax.dot_general(a, b, ((dims[:1], dims[1:]), ((), ())), preferred_element_type=F32)


def sigmoid(x):
    return 0.5 * jnp.tanh(0.5 * x) + 0.5


def lane_iota(shape):
    return lax.broadcasted_iota(jnp.int32, shape, len(shape) - 1)


def swap_halves(a, b):
    low = lane_iota(a.shape) < 64
    return jnp.where(low, a, pltpu.roll(b, 64, 1)), jnp.where(low, pltpu.roll(a, 64, 1), b)


def call(kernel, out_shape, scratch=(), vmem=16, flops=0, nbytes=0, trans=0, **kw):
    return pl.pallas_call(
        kernel,
        out_shape=out_shape,
        scratch_shapes=list(scratch),
        compiler_params=pltpu.CompilerParams(vmem_limit_bytes=vmem * MIB),
        cost_estimate=pl.CostEstimate(flops=flops, bytes_accessed=nbytes, transcendentals=trans),
        **kw,
    )


VM = pl.BlockSpec(memory_space=pltpu.VMEM)
SM = pl.BlockSpec(memory_space=pltpu.SMEM)
ANY = pl.BlockSpec(memory_space=pl.ANY)


def pack_kernel(after_ref, single_ref, noisy_ref, out_ref, scr):
    core = lax.axis_index("core")
    rows = single_ref[pl.ds(pl.multiple_of(32 * core, 32), 32), :]
    scr[...] = jnp.zeros_like(scr)
    for c in range(3):
        scr[0, 4 * c : 4 * c + 4, 0:64] = noisy_ref[c]
    x = scr[0]
    high = x.astype(BF16).astype(F32)
    rest = x - high
    mid = rest.astype(BF16).astype(F32)
    low = rest - mid
    parts = [part.astype(BF16) for part in (high, mid, low)]
    for n in range(out_ref.shape[0]):
        out_ref[n, 0:32, :] = rows
        for k in range(3):
            out_ref[n, 32:48, 128 * k : 128 * (k + 1)] = parts[k]


def pair_rows(idx_s, chain_s, idx_v, chain_v, x_scr, table_ref):
    row_dev = lax.axis_index("dap")
    base = 32 * (2 * lax.axis_index("sch") + lax.axis_index("core"))
    lane = lane_iota((1, 128))
    odd = (row_dev % 2) == 1

    def rows_of(ref):
        row = ref[pl.ds(row_dev // 2, 1), :]
        turned = pltpu.roll(row, 64, 1)
        return jnp.where(lane < 64, jnp.where(odd, turned, row), jnp.where(odd, row, turned))

    idx_i, chain_i = rows_of(idx_v), rows_of(chain_v)
    bin_ids = lax.broadcasted_iota(jnp.int32, (table_ref.shape[0], 128), 0)

    def block(n):
        embed, rows = [], []
        for m in (2 * n, 2 * n + 1):
            idx_k = jnp.where(lane < 64, idx_s[base + m], idx_s[base + 16 + m])
            chain_k = jnp.where(lane < 64, chain_s[base + m], chain_s[base + 16 + m])
            bins = jnp.where(chain_i == chain_k, jnp.clip(idx_i - idx_k, -32, 32) + 32, 65)
            embed.append((bin_ids == bins).astype(F32).astype(BF16))
            rows += [x_scr[:, m, :], x_scr[:, 16 + m, :]]
        pin = jnp.concatenate(rows, axis=0) + dot(jnp.concatenate(embed, axis=1), table_ref[...], (0, 0))
        center = pin - jnp.mean(pin, axis=-1, keepdims=True)
        spread = jnp.mean(center * center, axis=-1, keepdims=True)
        return pin, (center * lax.rsqrt(spread + 1e-5)).astype(BF16)

    return block


def pair_kernel(idx_s, chain_s, idx_v, chain_v, pair_ref, table_ref, proj_ref, msg_ref, x_scr, msg_scr):
    x_scr[...] = pair_ref[...].astype(F32)
    proj_t = jnp.transpose(proj_ref[...].astype(F32)).astype(BF16)
    block = pair_rows(idx_s, chain_s, idx_v, chain_v, x_scr, table_ref)
    for n in range(8):
        _, norm = block(n)
        projected = dot(proj_t, norm, (1, 1))
        left = sigmoid(projected[128:256]) * projected[0:128]
        right = sigmoid(projected[384:512]) * projected[256:384]
        for half in range(2):
            cols = slice(128 * half, 128 * half + 128)
            msg_scr[:, 2 * n + half, :] = left[:, cols]
            msg_scr[:, 16 + 2 * n + half, :] = right[:, cols]
    msg_ref[...] = msg_scr[...].astype(BF16)


def gate_kernel(after_ref, idx_s, chain_s, idx_v, chain_v, pair_ref, table_ref, gate_w_ref, pin_ref, gate_ref, x_scr):
    x_scr[...] = pair_ref[...].astype(F32)
    block = pair_rows(idx_s, chain_s, idx_v, chain_v, x_scr, table_ref)
    for n in range(8):
        pin, norm = block(n)
        pin_ref[n] = pin
        gate_ref[n] = sigmoid(dot(norm, gate_w_ref[...], (1, 0)))


def tri_kernel(msg_ref, after_ref, after2_ref, out_ref, even_l, odd_l, even_r, odd_r):
    for pair in range(4):
        for which, (even, odd) in enumerate(((even_l, odd_l), (even_r, odd_r))):
            a = msg_ref[32 * pair : 32 * pair + 16, 16 * which : 16 * which + 16, :]
            b = msg_ref[32 * pair + 16 : 32 * pair + 32, 16 * which : 16 * which + 16, :]
            a = a.astype(F32).reshape(256, 128)
            b = b.astype(F32).reshape(256, 128)
            low, high = swap_halves(a, b)
            even[:, 128 * pair : 128 * pair + 128] = low.astype(BF16)
            odd[:, 128 * pair : 128 * pair + 128] = high.astype(BF16)
    for pair in range(4):
        cols = slice(128 * pair, 128 * pair + 128)
        total = dot(even_r[...], even_l[:, cols], (0, 0)) + dot(odd_r[...], odd_l[:, cols], (0, 0))
        total = total.reshape(16, 2, 16, 128)
        a = total[:, 0].reshape(256, 128)
        b = total[:, 1].reshape(256, 128)
        low, high = swap_halves(a, b)
        out_ref[32 * pair : 32 * pair + 16] = low.reshape(16, 16, 128).astype(BF16)
        out_ref[32 * pair + 16 : 32 * pair + 32] = high.reshape(16, 16, 128).astype(BF16)


def update_kernel(tri_ref, pin_ref, gate_ref, tri_out_ref, bias_w_ref, after_ref, next_ref, bias_ref, t_scr, x_scr, b_scr):
    t_scr[...] = tri_ref[...].astype(F32)
    for n in range(8):
        tri = jnp.concatenate([t_scr[:, 2 * n, :], t_scr[:, 2 * n + 1, :]], axis=1)
        center = tri - jnp.mean(tri, axis=0, keepdims=True)
        spread = jnp.mean(center * center, axis=0, keepdims=True)
        norm = (center * lax.rsqrt(spread + 1e-5)).astype(BF16)
        update = dot(norm, tri_out_ref[...], (0, 0))
        new = (pin_ref[n] + gate_ref[n] * update).astype(BF16).astype(F32)
        for half in range(2):
            x_scr[:, 2 * n + half, :] = new[128 * half : 128 * half + 64]
            x_scr[:, 16 + 2 * n + half, :] = new[128 * half + 64 : 128 * half + 128]
        center = new - jnp.mean(new, axis=-1, keepdims=True)
        spread = jnp.mean(center * center, axis=-1, keepdims=True)
        norm = (center * lax.rsqrt(spread + 1e-5)).astype(BF16)
        bias = dot(bias_w_ref[...], norm, (1, 1)) * LOG2E
        for half in range(2):
            b_scr[:, 2 * n + half, :] = bias[:, 128 * half : 128 * half + 128]
    next_ref[...] = x_scr[...].astype(BF16)
    for head in range(16):
        block = b_scr[head].astype(BF16)
        for group in range(8):
            bias_ref[head // 2, group, head % 2] = block


def front_kernel(after_ref, types_ref, recv_ref, type_table_ref, single_w_ref, pos_w_ref, attn_w_ref,
                 q_ref, k_ref, v_ref, g_ref, cond_scr, w_scr, coord_scr, pos_scr):
    step = pl.program_id(0)
    width = pos_w_ref.shape[1]

    @pl.when(step == 0)
    def _():
        head = 2 * lax.axis_index("dap") + lax.axis_index("core")
        pick_row = lax.broadcasted_iota(jnp.int32, (48, width), 0)
        pick = (lane_iota((48, width)) == pick_row + 48 * head).astype(F32).astype(BF16)
        for n in range(4):
            w_scr[48 * n : 48 * n + 48, :] = dot(pick, attn_w_ref[:, width * n : width * (n + 1)], (1, 1)).astype(BF16)
        hot = (lax.broadcasted_iota(jnp.int32, (32, 512), 0) == types_ref[...]).astype(F32).astype(BF16)
        types = dot(hot, type_table_ref[...], (0, 0))
        for d in range(16):
            feat = recv_ref[d, 0:32, :].astype(F32) + types[32 * d : 32 * d + 32]
            center = feat - jnp.mean(feat, axis=-1, keepdims=True)
            spread = jnp.mean(center * center, axis=-1, keepdims=True)
            norm = (center * lax.rsqrt(spread + 1e-5)).astype(BF16)
            cond = dot(norm, single_w_ref[...], (1, 0))
            cond_scr[32 * d : 32 * d + 32, :] = cond - jnp.mean(cond, axis=-1, keepdims=True)
        for core in range(2):
            for pair in range(4):
                for part in range(3):
                    cols = slice(128 * part, 128 * part + 128)
                    a = recv_ref[4 * pair + core, 32:48, cols].astype(F32)
                    b = recv_ref[4 * pair + 2 + core, 32:48, cols].astype(F32)
                    both = jnp.where(lane_iota((16, 128)) < 64, a, pltpu.roll(b, 64, 1)).astype(BF16)
                    for term, own in enumerate((0, 0, 1, 1, 0, 2)):
                        if own == part:
                            coord_scr[core, 16 * term : 16 * term + 16, 128 * pair : 128 * pair + 128] = both
        pos = pos_w_ref[...]
        pos = pos - jnp.mean(pos, axis=-1, keepdims=True)
        high = pos.astype(BF16).astype(F32)
        mid = (pos - high).astype(BF16).astype(F32)
        low = pos - high - mid
        low = low.astype(BF16).astype(F32)
        pos_scr[...] = jnp.zeros_like(pos_scr)
        for term, own in enumerate((0, 1, 0, 1, 2, 0)):
            for c in range(3):
                start = 16 * term + 4 * c
                pos_scr[start : start + 4, :] = jnp.broadcast_to((high, mid, low)[own][c : c + 1], (4, width))

    core, smp = step // 4, step % 4
    row = lax.broadcasted_iota(jnp.int32, (96, width), 0)
    chosen = jnp.where((row & 3) == smp, pos_scr[...], 0.0).astype(BF16)
    act = cond_scr[...] + dot(coord_scr[core], chosen, (0, 0))
    spread = jnp.mean(act * act, axis=-1, keepdims=True)
    norm = (act * lax.rsqrt(spread + 1e-5)).astype(BF16)
    mixed = dot(w_scr[...], norm, (1, 1))
    q_ref[0] = mixed[0:48].astype(BF16)
    k_ref[0] = jnp.transpose(mixed[48:96]).astype(BF16)
    v_ref[0] = mixed[96:144].astype(BF16)
    g_ref[0] = sigmoid(mixed[144:192])


def attn_kernel(bias_in_ref, q_ref, k_ref, v_ref, g_ref, out_ref, bias_scr):
    @pl.when(pl.program_id(0) == 0)
    def _():
        for pair in range(4):
            a = bias_in_ref[32 * pair : 32 * pair + 16].astype(F32).reshape(256, 128)
            b = bias_in_ref[32 * pair + 16 : 32 * pair + 32].astype(F32).reshape(256, 128)
            low, high = swap_halves(a, b)
            bias_scr[:, 0, :, 128 * pair : 128 * pair + 128] = low.reshape(16, 16, 128)
            bias_scr[:, 1, :, 128 * pair : 128 * pair + 128] = high.reshape(16, 16, 128)

    scale = 48.0 ** (-0.5) * LOG2E
    for half in range(2):
        cols = slice(256 * half, 256 * half + 256)
        bias = bias_scr[:, :, :, cols].reshape(512, 256)
        gated = []
        for n in range(2):
            scores = dot(k_ref[n], q_ref[n, :, cols], (1, 0)) * scale + bias
            top = jnp.max(scores, axis=0, keepdims=True)
            weights = jnp.exp2(scores - top)
            total = jnp.sum(weights, axis=0, keepdims=True)
            mixed = dot(v_ref[n], weights.astype(BF16), (1, 0))
            gated.append(g_ref[n, :, cols] * (mixed / total))
        for pair in range(2):
            low, high = swap_halves(*[g[:, 128 * pair : 128 * pair + 128] for g in gated])
            out_ref[4 * half + 2 * pair, 0] = low.astype(BF16)
            out_ref[4 * half + 2 * pair + 1, 0] = high.astype(BF16)


def tail_kernel(gated_ref, act0_ref, noisy_ref, attn_out_ref, ff_gate_ref, ff_up_ref, ff_out_ref, coord_ref,
                out_ref, act_scr, norm_scr):
    step = pl.program_id(0)

    @pl.when(step == 0)
    def _():
        act = act0_ref[...] + dot(gated_ref[...], attn_out_ref[...], (0, 0))
        act_scr[...] = act
        center = act - jnp.mean(act, axis=-1, keepdims=True)
        spread = jnp.mean(center * center, axis=-1, keepdims=True)
        norm_scr[...] = (center * lax.rsqrt(spread + 1e-5)).astype(BF16)

    norm = norm_scr[...]
    gate = dot(norm, ff_gate_ref[...], (1, 0))
    up = dot(norm, ff_up_ref[...], (1, 0))
    inner = (gate * sigmoid(gate) * up).astype(BF16)
    act_scr[...] += dot(inner, ff_out_ref[...], (1, 0))

    @pl.when(step == pl.num_programs(0) - 1)
    def _():
        act = act_scr[...]
        center = act - jnp.mean(act, axis=-1, keepdims=True)
        spread = jnp.mean(center * center, axis=-1, keepdims=True)
        final = (center * lax.rsqrt(spread + 1e-5)).astype(BF16)
        shift = dot(coord_ref[...], final, (1, 1))
        for c in range(3):
            moves = [shift[c : c + 1, 64 * n : 64 * n + 64] for n in range(4)]
            out_ref[c] = noisy_ref[c] + jnp.concatenate(moves, axis=0)


def layer_norm(values):
    center = values - jnp.mean(values, axis=-1, keepdims=True)
    spread = jnp.mean(center * center, axis=-1, keepdims=True)
    return center * lax.rsqrt(spread + 1e-05)


def condition_rows(single_rows, type_rows, type_table, single_proj):
    type_ids = jnp.arange(type_table.shape[0], dtype=jnp.int32)
    type_hot = (type_rows[:, None] == type_ids[None, :]).astype(BF16)
    token_feat = single_rows.astype(F32) + jnp.dot(type_hot, type_table, preferred_element_type=F32)
    return jnp.dot(layer_norm(token_feat).astype(BF16), single_proj, preferred_element_type=F32)


def local(
    pair_rep,
    single,
    residue_type,
    chain_id,
    residue_index,
    noisy_pos,
    type_table,
    relpos_table,
    tri_proj,
    tri_gate,
    tri_out,
    bias_proj,
    single_proj,
    pos_proj,
    attn_proj,
    attn_out,
    ff_in,
    ff_out,
    coord_out,
):
    sds = jax.ShapeDtypeStruct
    dap = lax.axis_index("dap")
    noisy = noisy_pos.transpose(1, 0, 2)

    rows_in = (residue_index, chain_id, residue_index.reshape(4, 128), chain_id.reshape(4, 128), pair_rep, relpos_table)
    rows_specs = [SM, SM, VM, VM, VM, VM]
    msg = call(
        pair_kernel, sds((128, 32, 128), BF16),
        [pltpu.VMEM((64, 32, 128), F32), pltpu.VMEM((128, 32, 128), F32)],
        flops=400_000_000, nbytes=1_700_000, trans=600_000,
        in_specs=rows_specs + [VM], out_specs=VM,
    )(*rows_in, tri_proj)
    by_channel = lax.all_to_all(msg, AXES, 0, 0, tiled=True)

    packed = call(
        pack_kernel, sds((16, 48, 384), BF16), [pltpu.VMEM((1, 16, 128), F32)], nbytes=700_000,
        in_specs=[ANY, VM, VM], out_specs=VM,
    )(msg, single, noisy)
    inputs_all = lax.all_to_all(packed, ("dap", "core"), 0, 0, tiled=True)
    pair_in, gates = call(
        gate_kernel, (sds((8, 256, 128), F32), sds((8, 256, 128), F32)), [pltpu.VMEM((64, 32, 128), F32)],
        flops=130_000_000, nbytes=3_000_000, trans=300_000,
        in_specs=[ANY] + rows_specs + [VM], out_specs=(VM, VM),
    )(msg, *rows_in, tri_gate)

    tri = call(
        tri_kernel, sds((128, 16, 128), BF16), [pltpu.VMEM((256, 512), BF16)] * 4,
        flops=270_000_000, nbytes=1_500_000, in_specs=[VM, ANY, ANY], out_specs=VM,
    )(by_channel, inputs_all, pair_in)
    tri_back = lax.all_to_all(tri, AXES, 0, 0, tiled=True)

    whole = lambda shape: pl.BlockSpec(shape, lambda i: (0,) * len(shape))
    per = lambda *shape: pl.BlockSpec((1,) + shape, lambda i: (i, 0, 0))
    query, key, value, head_gates = call(
        front_kernel,
        (sds((8, 48, 512), BF16), sds((8, 512, 48), BF16), sds((8, 48, 512), BF16), sds((8, 48, 512), F32)),
        [pltpu.VMEM((512, 768), F32), pltpu.VMEM((192, 768), BF16), pltpu.VMEM((2, 96, 512), BF16),
         pltpu.VMEM((96, 768), F32)],
        vmem=32, flops=2_500_000_000, nbytes=8_000_000, trans=300_000,
        grid=(8,),
        in_specs=[ANY, whole((1, 512)), whole((16, 48, 384)), whole((32, 384)), whole((384, 768)), whole((3, 768)),
                  whole((768, 3072))],
        out_specs=(per(48, 512), per(512, 48), per(48, 512), per(48, 512)),
    )(tri, residue_type.reshape(1, 512), inputs_all, type_table, single_proj, pos_proj, attn_proj)

    pair_next, bias = call(
        update_kernel,
        (sds((64, 32, 128), BF16), sds((8, 8, 2, 16, 128), BF16)),
        [pltpu.VMEM((128, 16, 128), F32), pltpu.VMEM((64, 32, 128), F32), pltpu.VMEM((16, 16, 128), F32)],
        flops=80_000_000, nbytes=4_000_000, in_specs=[VM] * 5 + [ANY], out_specs=(VM, VM),
    )(tri_back, pair_in, gates, tri_out, bias_proj.T, query)
    bias_all = lax.all_to_all(bias.reshape(128, 16, 128), AXES, 0, 0, tiled=True)

    two = lambda *shape: pl.BlockSpec((2,) + shape, lambda i: (i, 0, 0))
    gated = call(
        attn_kernel, sds((8, 2, 48, 256), BF16), [pltpu.VMEM((16, 2, 16, 512), F32)],
        flops=1_000_000_000, nbytes=2_500_000, trans=2_100_000,
        grid=(4,),
        in_specs=[whole((128, 16, 128)), two(48, 512), two(512, 48), two(48, 512), two(48, 512)],
        out_specs=pl.BlockSpec((8, 1, 48, 128), lambda i: (0, i // 2, 0, i % 2)),
    )(bias_all, query, key, value, head_gates)
    gated_rows = lax.all_to_all(gated.reshape(16, 48, 256), ("dap", "core"), 0, 0, tiled=True).reshape(768, 256)

    type_rows = lax.dynamic_slice_in_dim(residue_type, dap * 64, 64)
    condition = condition_rows(single, type_rows, type_table, single_proj)
    act0 = condition[None] + jnp.einsum("scn,ct->snt", noisy_pos, pos_proj, precision=lax.Precision.HIGHEST)
    chunk = 512
    positions = call(
        tail_kernel, sds((3, 4, 64), F32), [pltpu.VMEM((256, 768), F32), pltpu.VMEM((256, 768), BF16)],
        vmem=20, flops=2_100_000_000, nbytes=9_500_000, trans=400_000,
        grid=(1536 // chunk,),
        in_specs=[whole((768, 256)), whole((256, 768)), whole((3, 4, 64)), whole((768, 768)),
                  pl.BlockSpec((768, chunk), lambda i: (0, i)),
                  pl.BlockSpec((768, chunk), lambda i: (0, i + 1536 // chunk)),
                  pl.BlockSpec((chunk, 768), lambda i: (i, 0)),
                  whole((3, 768))],
        out_specs=whole((3, 4, 64)),
    )(gated_rows, act0.reshape(256, 768), noisy, attn_out, ff_in, ff_in, ff_out, coord_out)
    return (pair_next, positions.transpose(1, 0, 2))


def solution(mesh):
    fine = Mesh(mesh.devices.reshape(8, 8, 2), AXES)
    rep = P()
    samp = ("sch", "core")
    in_specs = (P("dap", samp, None), P("dap", None), rep, rep, rep, P(samp, None, "dap")) + (rep,) * 13
    out_specs = (P("dap", samp, None), P(samp, None, "dap"))
    return jax.shard_map(local, mesh=fine, in_specs=in_specs, out_specs=out_specs, check_vma=False)
```

```python
import jax
import jax.numpy as jnp
from jax import lax
from jax.experimental import pallas as pl
from jax.experimental.pallas import tpu as pltpu
from jax.sharding import Mesh, PartitionSpec as P

F32 = jnp.float32
BF16 = jnp.bfloat16
AXES = ("dap", "sch", "core")
LOG2E = 1.4426950408889634
MIB = 1024 * 1024


def dot(a, b, dims):
    return lax.dot_general(a, b, ((dims[:1], dims[1:]), ((), ())), preferred_element_type=F32)


def sigmoid(x):
    return 0.5 * jnp.tanh(0.5 * x) + 0.5


def lane_iota(shape):
    return lax.broadcasted_iota(jnp.int32, shape, len(shape) - 1)


def swap_halves(a, b):
    low = lane_iota(a.shape) < 64
    return jnp.where(low, a, pltpu.roll(b, 64, 1)), jnp.where(low, pltpu.roll(a, 64, 1), b)


def call(kernel, out_shape, scratch=(), near=(), flops=0, nbytes=0, trans=0, **kw):
    run = pl.pallas_call(
        kernel,
        out_shape=out_shape,
        scratch_shapes=list(scratch),
        compiler_params=pltpu.CompilerParams(vmem_limit_bytes=40 * MIB),
        cost_estimate=pl.CostEstimate(flops=flops, bytes_accessed=nbytes, transcendentals=trans),
        **kw,
    )

    def far(*args):
        return run(*[x if n in near else pltpu.with_memory_space_constraint(x, pltpu.HBM) for n, x in enumerate(args)])

    return far


VM = pl.BlockSpec(memory_space=pltpu.VMEM)
SM = pl.BlockSpec(memory_space=pltpu.SMEM)
ANY = pl.BlockSpec(memory_space=pl.ANY)


def pack_kernel(after_ref, single_ref, noisy_ref, out_ref, own_ref, scr):
    scr[...] = jnp.zeros_like(scr)
    for c in range(3):
        scr[4 * c : 4 * c + 4, 0:64] = noisy_ref[c]
    x = scr[...]
    high = x.astype(BF16).astype(F32)
    rest = x - high
    mid = rest.astype(BF16).astype(F32)
    parts = [part.astype(BF16) for part in (high, mid, rest - mid)]
    out_ref[0:64, :] = single_ref[...]
    for k in range(3):
        out_ref[64:80, 128 * k : 128 * (k + 1)] = parts[k]
        own_ref[:, 128 * k : 128 * (k + 1)] = parts[k]


def pair_rows(idx_s, chain_s, idx_v, chain_v, x_scr, table_ref):
    row_dev = lax.axis_index("dap")
    base = 32 * (2 * lax.axis_index("sch") + lax.axis_index("core"))
    lane = lane_iota((1, 128))
    odd = (row_dev % 2) == 1

    def rows_of(ref):
        row = ref[pl.ds(row_dev // 2, 1), :]
        turned = pltpu.roll(row, 64, 1)
        return jnp.where(lane < 64, jnp.where(odd, turned, row), jnp.where(odd, row, turned))

    idx_i, chain_i = rows_of(idx_v), rows_of(chain_v)
    bin_ids = lax.broadcasted_iota(jnp.int32, (table_ref.shape[0], 128), 0)

    def block(n):
        embed, rows = [], []
        for m in (2 * n, 2 * n + 1):
            idx_k = jnp.where(lane < 64, idx_s[base + m], idx_s[base + 16 + m])
            chain_k = jnp.where(lane < 64, chain_s[base + m], chain_s[base + 16 + m])
            bins = jnp.where(chain_i == chain_k, jnp.clip(idx_i - idx_k, -32, 32) + 32, 65)
            embed.append((bin_ids == bins).astype(F32).astype(BF16))
            rows += [x_scr[m], x_scr[16 + m]]
        pin = jnp.concatenate(rows, axis=0) + dot(jnp.concatenate(embed, axis=1), table_ref[...], (0, 0))
        center = pin - jnp.mean(pin, axis=-1, keepdims=True)
        spread = jnp.mean(center * center, axis=-1, keepdims=True)
        return pin, (center * lax.rsqrt(spread + 1e-5)).astype(BF16)

    return block


def pair_kernel(idx_s, chain_s, idx_v, chain_v, pair_ref, table_ref, proj_ref, msg_ref, x_scr, msg_scr):
    x_scr[...] = jnp.swapaxes(pair_ref[...].astype(F32), 0, 1)
    proj_t = jnp.transpose(proj_ref[...].astype(F32)).astype(BF16)
    block = pair_rows(idx_s, chain_s, idx_v, chain_v, x_scr, table_ref)
    for n in range(8):
        _, norm = block(n)
        projected = dot(proj_t, norm, (1, 1))
        left = sigmoid(projected[128:256]) * projected[0:128]
        right = sigmoid(projected[384:512]) * projected[256:384]
        for half in range(2):
            cols = slice(128 * half, 128 * half + 128)
            msg_scr[2 * n + half] = left[:, cols]
            msg_scr[16 + 2 * n + half] = right[:, cols]
    msg_ref[...] = jnp.swapaxes(msg_scr[...], 0, 1).astype(BF16)


def gate_kernel(after_ref, idx_s, chain_s, idx_v, chain_v, pair_ref, table_ref, gate_w_ref, pin_ref, gate_ref, x_scr):
    x_scr[...] = jnp.swapaxes(pair_ref[...].astype(F32), 0, 1)
    block = pair_rows(idx_s, chain_s, idx_v, chain_v, x_scr, table_ref)
    for n in range(8):
        pin, norm = block(n)
        pin_ref[n] = pin
        gate_ref[n] = sigmoid(dot(norm, gate_w_ref[...], (1, 0)))


def tri_kernel(msg_ref, *refs):
    out_ref, even_l, odd_l, even_r, odd_r = refs[-5:]
    for pair in range(4):
        for which, (even, odd) in enumerate(((even_l, odd_l), (even_r, odd_r))):
            a = msg_ref[32 * pair : 32 * pair + 16, 16 * which : 16 * which + 16, :]
            b = msg_ref[32 * pair + 16 : 32 * pair + 32, 16 * which : 16 * which + 16, :]
            a = a.astype(F32).reshape(256, 128)
            b = b.astype(F32).reshape(256, 128)
            low, high = swap_halves(a, b)
            even[:, 128 * pair : 128 * pair + 128] = low.astype(BF16)
            odd[:, 128 * pair : 128 * pair + 128] = high.astype(BF16)
    for pair in range(4):
        cols = slice(128 * pair, 128 * pair + 128)
        total = dot(even_r[...], even_l[:, cols], (0, 0)) + dot(odd_r[...], odd_l[:, cols], (0, 0))
        total = total.reshape(16, 2, 16, 128)
        a = total[:, 0].reshape(256, 128)
        b = total[:, 1].reshape(256, 128)
        low, high = swap_halves(a, b)
        out_ref[32 * pair : 32 * pair + 16] = low.reshape(16, 16, 128).astype(BF16)
        out_ref[32 * pair + 16 : 32 * pair + 32] = high.reshape(16, 16, 128).astype(BF16)


def update_kernel(tri_ref, pin_ref, gate_ref, tri_out_ref, bias_w_ref, after_ref, next_ref, bias_ref,
                  t_scr, x_scr, b_scr):
    t_scr[...] = jnp.swapaxes(tri_ref[...].astype(F32), 0, 1)
    for n in range(8):
        tri = jnp.concatenate([t_scr[2 * n], t_scr[2 * n + 1]], axis=1)
        center = tri - jnp.mean(tri, axis=0, keepdims=True)
        spread = jnp.mean(center * center, axis=0, keepdims=True)
        norm = (center * lax.rsqrt(spread + 1e-5)).astype(BF16)
        update = dot(norm, tri_out_ref[...], (0, 0))
        new = (pin_ref[n] + gate_ref[n] * update).astype(BF16).astype(F32)
        for half in range(2):
            x_scr[2 * n + half] = new[128 * half : 128 * half + 64]
            x_scr[16 + 2 * n + half] = new[128 * half + 64 : 128 * half + 128]
        center = new - jnp.mean(new, axis=-1, keepdims=True)
        spread = jnp.mean(center * center, axis=-1, keepdims=True)
        norm = (center * lax.rsqrt(spread + 1e-5)).astype(BF16)
        bias = dot(bias_w_ref[...], norm, (1, 1)) * LOG2E
        for half in range(2):
            b_scr[:, 2 * n + half, :] = bias[:, 128 * half : 128 * half + 128]
    next_ref[...] = jnp.swapaxes(x_scr[...], 0, 1).astype(BF16)
    for pair in range(8):
        low, high = swap_halves(b_scr[2 * pair], b_scr[2 * pair + 1])
        low, high = low.astype(BF16), high.astype(BF16)
        for n in range(bias_ref.shape[0]):
            bias_ref[n, pair, 0:16, :] = low
            bias_ref[n, pair, 16:32, :] = high


def weights_kernel(after_ref, attn_w_ref, wk_ref, wv_ref, w_scr, sems):
    width = attn_w_ref.shape[0]
    copies = []
    for n in range(2):
        cols = slice(width * (n + 1), width * (n + 2))
        copies.append(pltpu.make_async_copy(attn_w_ref.at[:, cols], w_scr.at[n], sems.at[n]))
        copies[n].start()
    copies[0].wait()
    for pair in range(8):
        cols = slice(128 * pair, 128 * pair + 96)
        wk_ref[:, cols] = w_scr[0, :, 96 * pair : 96 * pair + 96]
        wk_ref[:, 128 * pair + 96 : 128 * pair + 128] = jnp.zeros((width, 32), BF16)
    copies[1].wait()
    wv_ref[...] = jnp.transpose(w_scr[1].astype(F32)).astype(BF16)


def keys_values(act, norm_scr, wk_ref, wv_ref, k_ref, v_ref):
    spread = jnp.mean(act * act, axis=-1, keepdims=True)
    norm = (act * lax.rsqrt(spread + 1e-5)).astype(BF16)
    for d in range(8):
        for core in range(2):
            norm_scr[256 * core + 32 * d : 256 * core + 32 * d + 32, :] = norm[64 * d + 32 * core : 64 * d + 32 * core + 32]
    norm = norm_scr[...]
    for pair in range(4):
        keys = dot(norm, wk_ref[:, 256 * pair : 256 * pair + 256], (1, 0)).astype(BF16)
        k_ref[0, 2 * pair] = keys[:, 0:128]
        k_ref[0, 2 * pair + 1] = keys[:, 128:256]
    v_ref[0] = dot(wv_ref[...], norm, (1, 1)).astype(BF16)


def sample_act(smp, cond_ref, coord_ref, pos_ref):
    row = lax.broadcasted_iota(jnp.int32, pos_ref.shape, 0)
    chosen = jnp.where((row & 3) == smp, pos_ref[...], 0.0).astype(BF16)
    coords = jnp.concatenate([coord_ref[z] for z in range(4)], axis=1)
    return cond_ref[...] + dot(coords, chosen, (0, 0))


def own_rows(norm_scr):
    start = pl.multiple_of(32 * lax.axis_index("dap"), 32)
    return jnp.concatenate([norm_scr[pl.ds(start, 32), :], norm_scr[pl.ds(256 + start, 32), :]], axis=0)


def first_kernel(after_ref, types_ref, own_ref, swap_ref, type_table_ref, single_w_ref, pos_w_ref, wk_ref, wv_ref,
                 cond_ref, coord_ref, pos_ref, k_ref, v_ref, own_norm_ref, type_scr, norm_scr):
    step = pl.program_id(0)

    @pl.when(step == 0)
    def _():
        shared(types_ref, own_ref, swap_ref, type_table_ref, single_w_ref, pos_w_ref, cond_ref, coord_ref, pos_ref, type_scr)

    keys_values(sample_act(step, cond_ref, coord_ref, pos_ref), norm_scr, wk_ref, wv_ref, k_ref, v_ref)
    own_norm_ref[...] = own_rows(norm_scr)


def shared(types_ref, own_ref, swap_ref, type_table_ref, single_w_ref, pos_w_ref, cond_ref, coord_ref, pos_ref, type_scr):
    width = pos_w_ref.shape[1]
    hot = (lax.broadcasted_iota(jnp.int32, (32, 512), 0) == types_ref[...]).astype(F32).astype(BF16)
    type_scr[...] = dot(hot, type_table_ref[...], (0, 0))
    own_z, own_y = lax.axis_index("dap") // 2, lax.axis_index("dap") % 2
    own_core = lax.axis_index("core")
    low_half = lane_iota((16, 128)) < 64
    for turn in range(4):
        z = own_z ^ turn
        for swap, ref in enumerate((own_ref, swap_ref)):
            rows = pl.ds(pl.multiple_of(128 * z + 64 * (own_y ^ own_core ^ swap), 64), 64)
            feat = ref[turn, 0:64, :].astype(F32) + type_scr[rows, :]
            center = feat - jnp.mean(feat, axis=-1, keepdims=True)
            spread = jnp.mean(center * center, axis=-1, keepdims=True)
            norm = (center * lax.rsqrt(spread + 1e-5)).astype(BF16)
            cond = dot(norm, single_w_ref[...], (1, 0))
            cond_ref[rows, :] = cond - jnp.mean(cond, axis=-1, keepdims=True)
        own_first = (own_y ^ own_core) == 0
        for part in range(3):
            cols = slice(128 * part, 128 * part + 128)
            mine = own_ref[turn, 64:80, cols].astype(F32)
            mates = swap_ref[turn, 80:96, cols].astype(F32)
            first = jnp.where(own_first, mine, mates)
            second = jnp.where(own_first, mates, mine)
            both = jnp.where(low_half, first, pltpu.roll(second, 64, 1)).astype(BF16)
            for term, own in enumerate((0, 0, 1, 1, 0, 2)):
                if own == part:
                    coord_ref[z, 16 * term : 16 * term + 16, :] = both
    pos = pos_w_ref[...]
    pos = pos - jnp.mean(pos, axis=-1, keepdims=True)
    high = pos.astype(BF16).astype(F32)
    mid = (pos - high).astype(BF16).astype(F32)
    low = (pos - high - mid).astype(BF16).astype(F32)
    pos_ref[...] = jnp.zeros_like(pos_ref)
    for term, own in enumerate((0, 1, 0, 1, 2, 0)):
        for c in range(3):
            row = 16 * term + 4 * c
            pos_ref[row : row + 4, :] = jnp.broadcast_to((high, mid, low)[own][c : c + 1], (4, width))


def second_kernel(after_ref, k_before, v_before, cond_ref, coord_ref, pos_ref, wk_ref, wv_ref, own_norm_ref, attn_w_hbm,
                  k_ref, v_ref, q_ref, g_ref, norm_scr, own_scr, w_scr, sems):
    step = pl.program_id(0)
    width = wv_ref.shape[0]
    loads = [pltpu.make_async_copy(attn_w_hbm.at[:, 3 * width * n : 3 * width * n + width], w_scr.at[n], sems.at[n])
             for n in range(2)]

    @pl.when(step == 0)
    def _():
        for load in loads:
            load.start()
        own_scr[0:128, :] = own_norm_ref[...]

    keys_values(sample_act(2 + step, cond_ref, coord_ref, pos_ref), norm_scr, wk_ref, wv_ref, k_ref, v_ref)
    own_scr[pl.ds(pl.multiple_of(128 + 64 * step, 64), 64), :] = own_rows(norm_scr)

    @pl.when(step == 1)
    def _():
        own = own_scr[...]
        for load in loads:
            load.wait()
        g_ref[...] = sigmoid(dot(w_scr[1], own, (0, 1)))
        queries = dot(w_scr[0], own, (0, 1)) * (48.0 ** (-0.5) * LOG2E)
        top_rows = lax.broadcasted_iota(jnp.int32, (96, 128), 0) < 48
        low = lane_iota((96, 128)) < 64
        for pair in range(8):
            for two in range(2):
                block = queries[96 * pair : 96 * pair + 96, 128 * two : 128 * two + 128]
                turned = pltpu.roll(block, 64, 1)
                for odd in range(2):
                    first, second = (turned, block) if odd else (block, turned)
                    diagonal = jnp.where(top_rows, jnp.where(low, first, 0.0), jnp.where(low, 0.0, second))
                    q_ref[2 * two + odd, pair, 0:96, :] = diagonal.astype(BF16)
                    q_ref[2 * two + odd, pair, 96:128, :] = jnp.zeros((32, 128), BF16)


def attn_kernel(own_bias_ref, swap_bias_ref, k_ref, v_ref, q_ref, noisy_ref, coord_ref, g_hbm, act0_hbm, attn_out_hbm,
                ff_in_hbm, ff_out_hbm, out_ref, att_scr, g_ref, act0_ref, attn_out_ref, ff_in_ref, ff_out_ref, sems):
    step = pl.program_id(0)
    pairs = ((g_hbm, g_ref), (act0_hbm, act0_ref), (attn_out_hbm, attn_out_ref), (ff_in_hbm, ff_in_ref), (ff_out_hbm, ff_out_ref))
    loads = [pltpu.make_async_copy(a, b, sems.at[n]) for n, (a, b) in enumerate(pairs)]

    @pl.when(step == 0)
    def _():
        for load in loads:
            load.start()

    even = (step % 2) == 0
    straight = (lax.broadcasted_iota(jnp.int32, (96, 128), 0) < 48) == even
    mine = (lane_iota((96, 128)) < 64) == even
    own_core = lax.axis_index("core")
    chunks = []
    for swap, bias_ref in enumerate((own_bias_ref, swap_bias_ref)):
        for n in range(2):
            chunks.append((bias_ref, 4 * n, pl.ds(pl.multiple_of(256 * (own_core ^ swap) + 128 * n, 128), 128)))
    for pair in range(8):
        query = q_ref[0, pair]
        rows = slice(96 * pair, 96 * pair + 96)
        scores, tops = [], []
        for bias_ref, first, keys in chunks:
            bias = bias_ref[first : first + 4, pair].astype(F32).reshape(128, 128)
            part = dot(k_ref[0, pair, keys, :], query, (1, 0)) + bias
            scores.append(part)
            tops.append(jnp.max(part, axis=0, keepdims=True))
        top = jnp.maximum(jnp.maximum(tops[0], tops[1]), jnp.maximum(tops[2], tops[3]))
        mixed, total = 0.0, 0.0
        for part, (_, _, keys) in zip(scores, chunks):
            weights = jnp.exp2(part - top)
            total += jnp.sum(weights, axis=0, keepdims=True)
            mixed += dot(v_ref[0, rows, keys], weights.astype(BF16), (1, 0))
        attended = mixed / total
        attended = jnp.where(straight, attended, pltpu.roll(attended, 64, 1))
        att_scr[step // 2, rows, :] = jnp.where(mine, attended, att_scr[step // 2, rows, :])

    @pl.when(step == pl.num_programs(0) - 1)
    def _():
        for load in loads[:3]:
            load.wait()
        gated = (g_ref[...] * jnp.concatenate([att_scr[0], att_scr[1]], axis=1)).astype(BF16)
        act = act0_ref[...] + dot(gated, attn_out_ref[...], (0, 0))
        center = act - jnp.mean(act, axis=-1, keepdims=True)
        spread = jnp.mean(center * center, axis=-1, keepdims=True)
        norm = (center * lax.rsqrt(spread + 1e-5)).astype(BF16)
        loads[3].wait()
        loads[4].wait()
        for n in range(3):
            gate = dot(norm, ff_in_ref[:, 512 * n : 512 * n + 512], (1, 0))
            up = dot(norm, ff_in_ref[:, 1536 + 512 * n : 2048 + 512 * n], (1, 0))
            inner = (gate * sigmoid(gate) * up).astype(BF16)
            act = act + dot(inner, ff_out_ref[512 * n : 512 * n + 512, :], (1, 0))
        center = act - jnp.mean(act, axis=-1, keepdims=True)
        spread = jnp.mean(center * center, axis=-1, keepdims=True)
        final = (center * lax.rsqrt(spread + 1e-5)).astype(BF16)
        shift = dot(coord_ref[...], final, (1, 1))
        for c in range(3):
            moves = [shift[c : c + 1, 64 * n : 64 * n + 64] for n in range(4)]
            out_ref[c] = noisy_ref[c] + jnp.concatenate(moves, axis=0)


def layer_norm(values):
    center = values - jnp.mean(values, axis=-1, keepdims=True)
    spread = jnp.mean(center * center, axis=-1, keepdims=True)
    return center * lax.rsqrt(spread + 1e-05)


def condition_rows(single_rows, type_rows, type_table, single_proj):
    type_ids = jnp.arange(type_table.shape[0], dtype=jnp.int32)
    type_hot = (type_rows[:, None] == type_ids[None, :]).astype(BF16)
    token_feat = single_rows.astype(F32) + jnp.dot(type_hot, type_table, preferred_element_type=F32)
    return jnp.dot(layer_norm(token_feat).astype(BF16), single_proj, preferred_element_type=F32)


def local(
    pair_rep,
    single,
    residue_type,
    chain_id,
    residue_index,
    noisy_pos,
    type_table,
    relpos_table,
    tri_proj,
    tri_gate,
    tri_out,
    bias_proj,
    single_proj,
    pos_proj,
    attn_proj,
    attn_out,
    ff_in,
    ff_out,
    coord_out,
):
    sds = jax.ShapeDtypeStruct
    hbm = lambda shape, dtype: pltpu.HBM(shape, dtype)
    dap = lax.axis_index("dap")
    noisy = noisy_pos.transpose(1, 0, 2)

    rows_in = (residue_index, chain_id, residue_index.reshape(4, 128), chain_id.reshape(4, 128), pair_rep, relpos_table)
    rows_specs = [SM, SM, VM, VM, VM, VM]
    msg = call(
        pair_kernel, sds((128, 32, 128), BF16),
        [pltpu.VMEM((32, 64, 128), F32), pltpu.VMEM((32, 128, 128), F32)],
        flops=400_000_000, nbytes=1_700_000, trans=600_000,
        in_specs=rows_specs + [VM], out_specs=VM,
    )(*rows_in, tri_proj)
    by_channel = lax.all_to_all(msg, AXES, 0, 0, tiled=True)

    pair_in, gates = call(
        gate_kernel, (hbm((8, 256, 128), F32), hbm((8, 256, 128), F32)), [pltpu.VMEM((32, 64, 128), F32)],
        flops=130_000_000, nbytes=3_000_000, trans=300_000,
        in_specs=[ANY] + rows_specs + [VM], out_specs=(VM, VM),
    )(msg, *rows_in, tri_gate)
    packed, own_coords = call(
        pack_kernel, (sds((80, 384), BF16), sds((16, 384), BF16)), [pltpu.VMEM((16, 128), F32)], nbytes=200_000,
        in_specs=[ANY, VM, VM], out_specs=(VM, VM),
    )(msg, single, noisy)
    other_coords = lax.ppermute(own_coords, "core", [(0, 1), (1, 0)])
    block = jnp.concatenate([packed, other_coords], axis=0)
    pieces = [
        lax.ppermute(block, ("dap", "core"), [(n, n ^ (4 * turn + 2 * (n & 1))) for n in range(16)]) for turn in range(4)
    ]

    w_key, w_value = call(
        weights_kernel, (hbm((768, 1024), BF16), hbm((768, 768), BF16)),
        [pltpu.VMEM((2, 768, 768), BF16), pltpu.SemaphoreType.DMA((2,))], nbytes=5_000_000,
        in_specs=[ANY, ANY], out_specs=(VM, VM),
    )(msg, attn_proj)

    tri = call(
        tri_kernel, sds((128, 16, 128), BF16), [pltpu.VMEM((256, 512), BF16)] * 4,
        flops=270_000_000, nbytes=1_500_000, near=(0,), in_specs=[VM, ANY, ANY], out_specs=VM,
    )(by_channel, pair_in, w_key)
    tri_back = lax.all_to_all(tri, AXES, 0, 0, tiled=True)
    pieces, _ = lax.optimization_barrier((pieces, tri))
    fetched = jnp.stack(pieces)
    swapped = lax.ppermute(fetched, "core", [(0, 1), (1, 0)])

    whole = lambda shape: pl.BlockSpec(shape, lambda i: (0,) * len(shape))
    sample = lambda shape, skip=0: pl.BlockSpec((1,) + shape, lambda i: (i + skip,) + (0,) * len(shape))
    cond, coords, pos_rows, keys, values, own_norm = call(
        first_kernel,
        (hbm((512, 768), F32), hbm((4, 96, 128), BF16), hbm((96, 768), F32), hbm((4, 8, 512, 128), BF16),
         hbm((4, 768, 512), BF16), hbm((128, 768), BF16)),
        [pltpu.VMEM((512, 384), F32), pltpu.VMEM((512, 768), BF16)],
        flops=3_300_000_000, nbytes=9_000_000,
        grid=(2,),
        in_specs=[ANY, whole((1, 512)), whole((4, 96, 384)), whole((4, 96, 384)), whole((32, 384)), whole((384, 768)),
                  whole((3, 768)), whole((768, 1024)), whole((768, 768))],
        out_specs=(whole((512, 768)), whole((4, 96, 128)), whole((96, 768)), sample((8, 512, 128)), sample((768, 512)),
                   pl.BlockSpec((64, 768), lambda i: (i, 0))),
    )(tri, residue_type.reshape(1, 512), fetched, swapped, type_table, single_proj, pos_proj, w_key, w_value)

    pair_next, bias = call(
        update_kernel,
        (sds((64, 32, 128), BF16), sds((8, 8, 32, 128), BF16)),
        [pltpu.VMEM((16, 128, 128), F32), pltpu.VMEM((32, 64, 128), F32), pltpu.VMEM((16, 16, 128), F32)],
        flops=80_000_000, nbytes=4_000_000, near=(0,), in_specs=[VM] * 5 + [ANY], out_specs=(VM, VM),
    )(tri_back, pair_in, gates, tri_out, bias_proj.T, cond)
    bias_own = lax.all_to_all(bias, "sch", 0, 0, tiled=True)
    keys, values, queries, gates_own = call(
        second_kernel,
        (hbm((4, 8, 512, 128), BF16), hbm((4, 768, 512), BF16), hbm((4, 8, 128, 128), BF16), hbm((768, 256), F32)),
        [pltpu.VMEM((512, 768), BF16), pltpu.VMEM((256, 768), BF16), pltpu.VMEM((2, 768, 768), BF16),
         pltpu.SemaphoreType.DMA((2,))],
        flops=3_500_000_000, nbytes=12_000_000, trans=200_000,
        grid=(2,),
        in_specs=[ANY, ANY, ANY, whole((512, 768)), whole((4, 96, 128)), whole((96, 768)), whole((768, 1024)), whole((768, 768)),
                  whole((128, 768)), ANY],
        out_specs=(sample((8, 512, 128), 2), sample((768, 512), 2), whole((4, 8, 128, 128)), whole((768, 256))),
        input_output_aliases={1: 0, 2: 1},
    )(bias, keys, values, cond, coords, pos_rows, w_key, w_value, own_norm, attn_proj)
    bias_own, queries = lax.optimization_barrier((bias_own, queries))
    bias_swap = lax.ppermute(bias_own, "core", [(0, 1), (1, 0)])

    type_rows = lax.dynamic_slice_in_dim(residue_type, dap * 64, 64)
    condition = condition_rows(single, type_rows, type_table, single_proj)
    act0 = condition[None] + jnp.einsum("scn,ct->snt", noisy_pos, pos_proj, precision=lax.Precision.HIGHEST)
    positions = call(
        attn_kernel, sds((3, 4, 64), F32),
        [pltpu.VMEM((2, 768, 128), F32), pltpu.VMEM((768, 256), F32), pltpu.VMEM((256, 768), F32),
         pltpu.VMEM((768, 768), BF16), pltpu.VMEM((768, 3072), BF16), pltpu.VMEM((1536, 768), BF16),
         pltpu.SemaphoreType.DMA((5,))],
        near=(0, 1), flops=3_500_000_000, nbytes=18_000_000, trans=2_500_000,
        grid=(4,),
        in_specs=[whole((8, 8, 32, 128)), whole((8, 8, 32, 128)), sample((8, 512, 128)), sample((768, 512)),
                  sample((8, 128, 128)), whole((3, 4, 64)), whole((3, 768)), ANY, ANY, ANY, ANY, ANY],
        out_specs=whole((3, 4, 64)),
    )(bias_own, bias_swap, keys, values, queries, noisy, coord_out, gates_own, act0.reshape(256, 768), attn_out, ff_in, ff_out)
    return (pair_next, positions.transpose(1, 0, 2))


def solution(mesh):
    fine = Mesh(mesh.devices.reshape(8, 8, 2), AXES)
    rep = P()
    samp = ("sch", "core")
    in_specs = (P("dap", samp, None), P("dap", None), rep, rep, rep, P(samp, None, "dap")) + (rep,) * 13
    out_specs = (P("dap", samp, None), P(samp, None, "dap"))
    return jax.shard_map(local, mesh=fine, in_specs=in_specs, out_specs=out_specs, check_vma=False)
```
